32 devices in a mesh: sec: 4 (over x, core), tile: 8 (over z, y).
Axes of the slice: x: 2, y: 2, z: 4, core: 2. Of those that a mesh axis runs over, the one named last changes fastest.
Arguments:
- pixels: bfloat16 [16, 2048, 512], P('sec', 'tile'), may hold values from -6 to 6
- valid: int32 [16, 8], P('sec', 'tile'), may hold values 0 or 1
- offsets: int32 [16, 2, 64, 128], P('sec', None, 'tile'), may hold values from -64 to 63
- neighbours: int32 [16, 4, 64, 128], P('sec', None, 'tile'), may hold values from 0 to 1280, as said below
Outputs:
- ncc_maps: float32 [16, 8, 128, 128], P('sec', 'tile')
- displacement: float32 [16, 2, 64, 128], P('sec', None, 'tile')
The draws below stay inside these ranges and needn't reach their ends.
Inputs may be any that keep to these rules, and one draw needn't show every extreme that they name: `neighbours`: slot d of a node (d = 0, 1, 2, 3 for the directions x - 1, x + 1, y - 1, y + 1) either is (10) * 128, an empty slot, or names the node's grid neighbour in that direction as local_col * 128 + row, with local_col in [0, 10): columns 1 to 8 are the tile's own, 0 and 9 the adjacent edge columns of the neighbouring tiles.
All inputs are finite; a program needn't handle non-finite values. No bound on the sum of `valid` on one device may be relied on, other than what follows from the above.
Results may differ from the reference program's by a relative error of at most 0.0085.
Values may be sent and summed in bfloat16 or wider, within the bound.
A program may use at most 64 MiB of HBM per device.

```python
import math
from functools import partial
import jax
import jax.numpy as jnp
from jax import lax

PATCH = 512
HALO = 128
SHIFTS = 128
GX_DEV = 8
GY = 128
SWEEPS = 4
TILE_W = 256
SECTIONS = 16
PATCHES = 8
PIX_X = 2048
NODES_X = 64
N_TILE = 8


def section_shifts(key):
    key = jax.random.fold_in(key, 29)
    keys = jax.random.split(key, 2)
    reach = SHIFTS // 4
    shift_x = jax.random.randint(keys[0], (SECTIONS,), -reach, reach + 1)
    shift_y = jax.random.randint(keys[1], (SECTIONS,), -reach, reach + 1)
    return (shift_x, shift_y)


def draw_pixels(key, part):
    shift_x, shift_y = section_shifts(key)
    key = jax.random.fold_in(key, 11)
    keys = jax.random.split(key, 2)
    common = jax.random.normal(keys[0], (PIX_X, PATCH), jnp.float32)
    noise = jax.random.normal(keys[1], (SECTIONS, PIX_X, PATCH), jnp.float32)

    def moved(amount_x, amount_y):
        return jnp.roll(jnp.roll(common, amount_x, axis=0), amount_y, axis=1)
    image = 0.8 * jax.vmap(moved)(shift_x, shift_y) + 0.6 * noise
    return jnp.clip(image, -6.0, 6.0).astype(jnp.bfloat16)


def draw_offsets(key, part):
    shift_x, shift_y = section_shifts(key)
    key = jax.random.fold_in(key, 13)
    keys = jax.random.split(key, 3)
    half_win = SHIFTS // 2
    zero_one = jnp.zeros((1,), jnp.int32)
    step_x = jnp.concatenate([shift_x[1:] - shift_x[:-1], zero_one])
    step_y = jnp.concatenate([shift_y[1:] - shift_y[:-1], zero_one])
    base = jnp.stack([step_x, step_y], axis=1)[:, :, None, None]
    shape = (SECTIONS, 2, NODES_X, GY)
    base = jnp.broadcast_to(base, shape)
    sort_of = jax.random.randint(keys[0], (SECTIONS, 1, NODES_X, GY), 0, 4)
    jitter = jax.random.randint(keys[1], shape, -2, 3)
    spread = jax.random.randint(keys[2], shape, -half_win, half_win)
    value = jnp.where(sort_of == 3, spread, jnp.where(sort_of == 2, base + jitter, base))
    value = jnp.clip(value, -half_win, half_win - 1)
    value = value.at[0, 0, 0, 0].set(-half_win)
    value = value.at[0, 1, 0, 0].set(half_win - 1)
    return value.astype(jnp.int32)


def draw_neighbours(key, part):
    key = jax.random.fold_in(key, 7)
    xpos = jnp.arange(NODES_X, dtype=jnp.int32)[:, None]
    ypos = jnp.arange(GY, dtype=jnp.int32)[None, :]
    step_x = [-1, 1, 0, 0]
    step_y = [0, 0, -1, 1]
    limit = (GX_DEV + 2) * GY
    tables = []
    for direction in range(4):
        near_x = xpos + step_x[direction]
        near_y = ypos + step_y[direction]
        inside = (near_x >= 0) & (near_x < NODES_X) & (near_y >= 0) & (near_y < GY)
        local_col = xpos % GX_DEV + 1 + step_x[direction]
        tables.append(jnp.where(inside, local_col * GY + near_y, limit))
    table = jnp.stack(tables)[None]
    kept_edge = jax.random.randint(key, (SECTIONS, 4, NODES_X, GY), 0, 5) > 0
    return jnp.where(kept_edge, table, limit).astype(jnp.int32)


def with_ends(entries, key, low, top_value):
    longest = entries.shape.index(max(entries.shape))
    spots = []
    for shift in (0, 1):
        where = [jax.random.randint(jax.random.fold_in(key, axis), (), 0, length) for axis, length in enumerate(entries.shape)]
        where[longest] = (where[longest] + shift) % entries.shape[longest]
        spots.append(tuple(where))
    return entries.at[spots[0]].set(low).at[spots[1]].set(top_value)


def setup_inputs(seed: int = 0) -> dict:
    arg_keys = jax.random.split(jax.random.key(seed), 5)
    pixels = draw_pixels(jax.random.fold_in(arg_keys[4], 71), 0)
    valid = with_ends((jax.random.randint(arg_keys[1], (SECTIONS, PATCHES), 0, 4) < 3).astype(jnp.int32), jax.random.fold_in(arg_keys[1], 1), 0, 1)
    offsets = draw_offsets(jax.random.fold_in(arg_keys[4], 71), 0)
    neighbours = draw_neighbours(jax.random.fold_in(arg_keys[4], 71), 0)
    return {"pixels": pixels, "valid": valid, "offsets": offsets, "neighbours": neighbours}


EPS = 1e-06

def forward_tables():
    index = jnp.arange(PATCH, dtype=jnp.int32)
    product = index[:, None] * index[None, :] % PATCH
    angles = product.astype(jnp.float32) * (2.0 * math.pi / PATCH)
    return (jnp.cos(angles).astype(jnp.bfloat16), jnp.sin(angles).astype(jnp.bfloat16))

def offset_tables():
    shift_ids = jnp.arange(SHIFTS, dtype=jnp.int32) - SHIFTS // 2
    index = jnp.arange(PATCH, dtype=jnp.int32)
    product = shift_ids[:, None] * index[None, :] % PATCH
    angles = product.astype(jnp.float32) * (2.0 * math.pi / PATCH)
    return (jnp.cos(angles).astype(jnp.bfloat16), jnp.sin(angles).astype(jnp.bfloat16))

def spectrum(window_in, cos_tab, sin_tab):
    rows_re = jnp.dot(window_in, cos_tab, preferred_element_type=jnp.float32).astype(jnp.bfloat16)
    rows_im = (-jnp.dot(window_in, sin_tab, preferred_element_type=jnp.float32)).astype(jnp.bfloat16)
    full_re = jnp.dot(cos_tab, rows_re, preferred_element_type=jnp.float32) + jnp.dot(sin_tab, rows_im, preferred_element_type=jnp.float32)
    full_im = jnp.dot(cos_tab, rows_im, preferred_element_type=jnp.float32) - jnp.dot(sin_tab, rows_re, preferred_element_type=jnp.float32)
    return (full_re, full_im)

def similarity(own_re, own_im, energy_p, pair_re, pair_im, energy_q, cos_off, sin_off):
    cross_re = (own_re * pair_re + own_im * pair_im).astype(jnp.bfloat16)
    cross_im = (own_re * pair_im - own_im * pair_re).astype(jnp.bfloat16)
    half_re = (jnp.dot(cos_off, cross_re, preferred_element_type=jnp.float32) - jnp.dot(sin_off, cross_im, preferred_element_type=jnp.float32)).astype(jnp.bfloat16)
    half_im = (jnp.dot(cos_off, cross_im, preferred_element_type=jnp.float32) + jnp.dot(sin_off, cross_re, preferred_element_type=jnp.float32)).astype(jnp.bfloat16)
    correl = jnp.dot(half_re, cos_off.T, preferred_element_type=jnp.float32) - jnp.dot(half_im, sin_off.T, preferred_element_type=jnp.float32)
    volume = float(PATCH) ** 4
    return correl / volume / jnp.sqrt(energy_p * energy_q + EPS)

def displacement_field(ncc_maps, valid, offsets, neighbours):
    sec_total = offsets.shape[0]
    node_x = offsets.shape[2]
    half_win = SHIFTS // 2
    tile_of_x = jnp.arange(node_x, dtype=jnp.int32) // GX_DEV
    sec_ids = jnp.arange(sec_total, dtype=jnp.int32)
    matched = ncc_maps[sec_ids[:, None, None], tile_of_x[None, :, None], offsets[:, 0] + half_win, offsets[:, 1] + half_win]
    valid_f = valid[:, tile_of_x].astype(jnp.float32)[:, :, None]
    weight = (valid_f * (0.5 + 8.0 * (matched * matched)))[:, None]
    target = offsets.astype(jnp.float32) * (2.0 / SHIFTS)
    limit = (GX_DEV + 2) * GY
    linked = neighbours < limit
    degree = lax.optimization_barrier(jnp.sum(linked.astype(jnp.float32), axis=1, keepdims=True))
    column = neighbours // GY
    row_pos = neighbours % GY
    global_col = (tile_of_x * GX_DEV)[None, None, :, None] + column - 1
    inside = linked & (global_col >= 0) & (global_col < node_x)
    total = node_x * GY
    flat_idx = jnp.where(inside, global_col * GY + row_pos, 0).astype(jnp.int32).reshape(sec_total, 1, 4, total)
    flat_idx = jnp.broadcast_to(flat_idx, (sec_total, 2, 4, total))
    inside_b = jnp.broadcast_to(inside.reshape(sec_total, 1, 4, total), (sec_total, 2, 4, total))
    sec_count = ((sec_ids > 0).astype(jnp.float32) + (sec_ids < sec_total - 1).astype(jnp.float32))[:, None, None, None]
    displace = target
    for sweep_no in range(SWEEPS):
        disp_flat = jnp.broadcast_to(displace.reshape(sec_total, 2, 1, total), (sec_total, 2, 4, total))
        fetched = jnp.take_along_axis(disp_flat, flat_idx, axis=3)
        edge_sum = lax.optimization_barrier(jnp.sum(jnp.where(inside_b, fetched, jnp.float32(0.0)), axis=2)).reshape(displace.shape)
        sec_pad = jnp.pad(displace, ((1, 1), (0, 0), (0, 0), (0, 0)))
        sec_sum = sec_pad[:-2] + sec_pad[2:]
        displace = (edge_sum + sec_sum + weight * target) / (degree + sec_count + weight + 1.0)
    return displace

def reference(pixels, valid, offsets, neighbours):
    cos_tab, sin_tab = forward_tables()
    cos_off, sin_off = offset_tables()
    padded = jnp.pad(pixels, ((0, 0), (HALO, HALO), (0, 0)))

    def per_tile(tile_no):
        start = (tile_no * TILE_W).astype(jnp.int32)
        windows = lax.dynamic_slice_in_dim(padded, start, PATCH, axis=1)
        own_re, own_im = jax.vmap(partial(spectrum, cos_tab=cos_tab, sin_tab=sin_tab))(windows)
        energy = lax.optimization_barrier(jnp.mean(jnp.square(windows.astype(jnp.float32)), axis=(1, 2)))
        pair_re = jnp.concatenate([own_re[1:], jnp.zeros_like(own_re[:1])], axis=0)
        pair_im = jnp.concatenate([own_im[1:], jnp.zeros_like(own_im[:1])], axis=0)
        energy_q = jnp.concatenate([energy[1:], jnp.zeros((1,), jnp.float32)], axis=0)
        return jax.vmap(partial(similarity, cos_off=cos_off, sin_off=sin_off))(own_re, own_im, energy, pair_re, pair_im, energy_q)
    tile_maps = lax.map(per_tile, jnp.arange(N_TILE, dtype=jnp.int32))
    ncc_maps = jnp.transpose(tile_maps, (1, 0, 2, 3))
    return (ncc_maps, displacement_field(ncc_maps, valid, offsets, neighbours))
```

```python
import functools

import jax
import jax.numpy as jnp
import ml_dtypes
import numpy as np
from jax import lax
from jax.experimental import pallas as pl
from jax.experimental.pallas import tpu as pltpu
from jax.sharding import PartitionSpec as P

PATCH = 512
HALF = PATCH // 2
HALO = 128
SHIFTS = 128
SWEEPS = 4
EPS = 1e-06
F32 = jnp.float32
BF16 = jnp.bfloat16


def cos_sin(product):
    angles = (product % PATCH) * (2.0 * np.pi / PATCH)
    return np.cos(angles), np.sin(angles)


def tables():
    pos = np.arange(PATCH)
    freq = np.arange(HALF)
    cos, sin = cos_sin(pos[:, None] * freq[None, :])
    row_tab = np.concatenate([cos, -sin], axis=1)
    row_tab[:, HALF] = 1.0 - 2.0 * (pos % 2)
    col_tab = []
    for parity in (0, 1):
        cos, sin = cos_sin((2 * freq[:, None] + parity) * freq[None, :])
        col_tab.append(np.block([[cos, sin], [-sin, cos]]))
    shift = np.arange(SHIFTS) - SHIFTS // 2
    order = np.concatenate([2 * freq, 2 * freq + 1])
    cos, sin = cos_sin(shift[:, None] * order[None, :])
    off_tab = np.block([[cos, -sin], [sin, cos]])
    cos, sin = cos_sin(freq[:, None] * shift[None, :])
    twice = np.where(freq == 0, 1.0, 2.0)[:, None]
    map_tab = np.concatenate([cos * twice, -sin * twice], axis=0)
    return [
        np.asarray(a, np.float32).astype(ml_dtypes.bfloat16)
        for a in (row_tab, np.stack(col_tab), off_tab, map_tab)
    ]


def dot(a, b):
    return jnp.dot(a, b, preferred_element_type=F32)


def kernel(
    n_sec, n_tile,
    px, valid, off, nbr, row_hbm, col_hbm, offt_hbm, map_hbm,
    ncc_out, disp_out,
    win, offv, nbrv, row_tab, col_tab, off_tab, map_tab,
    own, mix, spec, cross, nyq, maps, energy, onehot,
    ext, wts, disp, live, inv, pull, first,
    loc_sem, halo_send, halo_recv, next_send, next_recv, ext_send, ext_recv, w_send, w_recv,
):
    sec = lax.axis_index("sec")
    tile = lax.axis_index("tile")
    secs = px.shape[0]
    width = px.shape[1]
    cols = off.shape[2]
    rows = off.shape[3]
    nxt = secs
    has_left, has_right = tile > 0, tile < n_tile - 1
    has_prev, has_next = sec > 0, sec < n_sec - 1
    sides = (
        (has_left, {"tile": tile - 1}),
        (has_right, {"tile": tile + 1}),
        (has_prev, {"sec": sec - 1}),
        (has_next, {"sec": sec + 1}),
    )

    def remote(src, dst, send, recv, to):
        return pltpu.make_async_remote_copy(
            src_ref=src, dst_ref=dst, send_sem=send, recv_sem=recv,
            device_id=to, device_id_type=pl.DeviceIdType.MESH,
        )

    barrier = pltpu.get_barrier_semaphore()
    for there, to in sides:
        @pl.when(there)
        def _(to=to):
            pl.semaphore_signal(barrier, inc=1, device_id=to, device_id_type=pl.DeviceIdType.MESH)

    local = [
        pltpu.make_async_copy(off, offv, loc_sem.at[0]),
        pltpu.make_async_copy(nbr, nbrv, loc_sem.at[1]),
        pltpu.make_async_copy(row_hbm, row_tab, loc_sem.at[2]),
        pltpu.make_async_copy(col_hbm, col_tab, loc_sem.at[3]),
        pltpu.make_async_copy(offt_hbm, off_tab, loc_sem.at[4]),
        pltpu.make_async_copy(map_hbm, map_tab, loc_sem.at[5]),
    ]
    mine = [
        pltpu.make_async_copy(px.at[s], win.at[s, pl.ds(HALO, width)], loc_sem.at[6 + s])
        for s in range(secs)
    ]
    pl.semaphore_wait(barrier, sum(there.astype(jnp.int32) for there, _ in sides))

    low = pl.ds(0, HALO)
    high = pl.ds(HALO + width, HALO)

    def halo_copy(s, side):
        if side == 0:
            return remote(px.at[s, pl.ds(0, HALO)], win.at[s, high],
                          halo_send.at[s, 0], halo_recv.at[s, 1], sides[0][1])
        return remote(px.at[s, pl.ds(width - HALO, HALO)], win.at[s, low],
                      halo_send.at[s, 1], halo_recv.at[s, 0], sides[1][1])

    def next_copy(part):
        if part == 0:
            src, dst = px.at[0], win.at[nxt, pl.ds(HALO, width)]
        else:
            place = low if part == 1 else high
            src, dst = win.at[0, place], win.at[nxt, place]
        return remote(src, dst, next_send.at[part], next_recv.at[part], sides[2][1])

    def ext_copy(side):
        if side < 2:
            src, dst = ext.at[1, 1], ext.at[1, 2 - 2 * side]
        else:
            src, dst = ext.at[1], ext.at[2 - 2 * (side - 2)]
        return remote(src, dst, ext_send.at[side], ext_recv.at[side ^ 1], sides[side][1])

    def w_copy(side):
        if side < 2:
            src, dst = wts.at[1, 1], wts.at[1, 2 - 2 * side]
        else:
            src, dst = wts.at[1], wts.at[2 - 2 * (side - 2)]
        return remote(src, dst, w_send.at[side], w_recv.at[side ^ 1], sides[side][1])

    def when(there, action):
        pl.when(there)(action)

    for s in range(secs):
        when(has_right, lambda: halo_copy(s, 1).start())
        when(has_left, lambda: halo_copy(s, 0).start())
        if s == 0:
            when(has_prev, lambda: next_copy(0).start())
    for copy in local + mine:
        copy.start()

    @pl.when(jnp.logical_not(has_left))
    def _():
        for s in range(secs):
            win[s, low] = jnp.zeros((HALO, PATCH), BF16)
        ext[1, 0] = jnp.zeros(ext.shape[2:], BF16)
        wts[1, 0] = jnp.zeros(wts.shape[2:], F32)

    @pl.when(jnp.logical_not(has_right))
    def _():
        for s in range(secs):
            win[s, high] = jnp.zeros((HALO, PATCH), BF16)
        ext[1, 2] = jnp.zeros(ext.shape[2:], BF16)
        wts[1, 2] = jnp.zeros(wts.shape[2:], F32)

    @pl.when(jnp.logical_not(has_prev))
    def _():
        ext[0] = jnp.zeros(ext.shape[1:], BF16)
        wts[0] = jnp.zeros(wts.shape[1:], F32)

    @pl.when(jnp.logical_not(has_next))
    def _():
        win[nxt] = jnp.zeros((PATCH, PATCH), BF16)
        ext[2] = jnp.zeros(ext.shape[1:], BF16)
        wts[2] = jnp.zeros(wts.shape[1:], F32)

    nyq[...] = jnp.zeros(nyq.shape, F32)

    local[0].wait()
    local[1].wait()
    limit = (cols + 2) * rows
    for s in range(secs):
        ext[1, 1, s, pl.ds(0, 2 * cols)] = offv[s].reshape(2 * cols, rows).astype(F32).astype(BF16)
        ext[1, 1, s, pl.ds(2 * cols, 4 * cols)] = jnp.where(
            nbrv[s].reshape(4 * cols, rows) < limit, F32(1.0), F32(0.0)).astype(BF16)
    when(has_left, lambda: ext_copy(0).start())
    when(has_right, lambda: ext_copy(1).start())

    local[2].wait()

    def own_rows(j):
        own[j] = dot(win[j, pl.ds(HALO, width)], row_tab[...])

    for s in range(secs):
        mine[s].wait()
        own_rows(s)

    half_win = SHIFTS // 2
    place = lax.broadcasted_iota(jnp.int32, (SHIFTS, rows), 0) - half_win

    def fill_onehot(s):
        for x in range(cols):
            hit = jnp.where(place == offv[s, 1, x:x + 1, :], F32(1.0), F32(0.0)).astype(BF16)
            onehot[s, pl.ds(0, SHIFTS), pl.ds(x * rows, rows)] = hit
            onehot[s, pl.ds(SHIFTS, SHIFTS), pl.ds(x * rows, rows)] = hit

    for s in range(secs):
        fill_onehot(s)
    for copy in local[3:]:
        copy.wait()

    lane = lax.broadcasted_iota(jnp.int32, (HALO, SHIFTS), 1)
    lane_wide = lax.broadcasted_iota(jnp.int32, (HALO, HALF), 1)

    def spectrum(j):
        pix = win[j].astype(F32)
        total = jnp.sum(jnp.sum(pix * pix, axis=0, keepdims=True), axis=1, keepdims=True)
        energy[j:j + 1, :] = jnp.broadcast_to(total * (1.0 / (PATCH * PATCH)), (1, SHIFTS))
        first_rows = dot(win[j, low], row_tab[...])
        last_rows = dot(win[j, high], row_tab[...])
        for part, (a, b) in enumerate((
            (first_rows, own[j, pl.ds(HALO, HALO)]),
            (own[j, pl.ds(0, HALO)], last_rows),
        )):
            for parity, value in enumerate((a + b, a - b)):
                mix[parity, pl.ds(part * HALO, HALO)] = value[:, :HALF].astype(BF16)
                mix[parity, pl.ds(HALF + part * HALO, HALO)] = jnp.where(
                    lane_wide == 0, F32(0.0), value[:, HALF:]).astype(BF16)
                at = (parity, pl.ds(part * HALO, HALO))
                nyq[at] = jnp.where(lane == j, value[:, HALF:HALF + 1], nyq[at])
        for parity in (0, 1):
            spec[j, parity] = dot(col_tab[parity], mix[parity])

    def cross_of(p_re, p_im, q_re, q_im):
        return (
            (p_re * q_re + p_im * q_im).astype(BF16),
            (p_re * q_im - p_im * q_re).astype(BF16),
        )

    def correlate(s):
        for parity in (0, 1):
            re, im = cross_of(
                spec[s, parity, pl.ds(0, HALF)], spec[s, parity, pl.ds(HALF, HALF)],
                spec[s + 1, parity, pl.ds(0, HALF)], spec[s + 1, parity, pl.ds(HALF, HALF)])
            cross[pl.ds(parity * HALF, HALF)] = re
            cross[pl.ds(PATCH + parity * HALF, HALF)] = im
        half = dot(off_tab[...], cross[...]).astype(BF16)
        maps[s] = dot(half[:SHIFTS], map_tab[pl.ds(0, HALF)]) + dot(
            half[SHIFTS:], map_tab[pl.ds(HALF, HALF)])

    def wait_halo(s):
        when(has_left, lambda: halo_copy(s, 1).wait_recv())
        when(has_right, lambda: halo_copy(s, 0).wait_recv())

    wait_halo(0)

    @pl.when(has_prev)
    def _():
        next_copy(1).start()
        next_copy(2).start()

    spectrum(0)
    when(has_right, lambda: ext_copy(0).wait_recv())
    when(has_left, lambda: ext_copy(1).wait_recv())
    when(has_prev, lambda: ext_copy(2).start())
    when(has_next, lambda: ext_copy(3).start())
    wait_halo(1)
    spectrum(1)
    correlate(0)

    @pl.when(has_next)
    def _():
        for part in range(3):
            next_copy(part).wait_recv()

    own_rows(nxt)
    spectrum(nxt)
    wait_halo(2)
    spectrum(2)
    correlate(1)

    when(has_prev, lambda: ext_copy(3).wait_recv())
    when(has_next, lambda: ext_copy(2).wait_recv())
    wide = 3 * cols
    for sb in range(3):
        for s in range(secs):
            at = sb * secs + s
            for tb in range(3):
                for c in range(2):
                    disp[0, at, c, pl.ds(tb * cols, cols)] = ext[
                        sb, tb, s, pl.ds(0, 2 * cols)].astype(F32)[
                            c * cols:(c + 1) * cols] * (2.0 / SHIFTS)
                for d in range(4):
                    live[at, d, pl.ds(tb * cols, cols)] = ext[
                        sb, tb, s, pl.ds(2 * cols, 4 * cols)].astype(F32)[d * cols:(d + 1) * cols]
    y = lax.broadcasted_iota(jnp.int32, (wide, rows), 1)
    x = lax.broadcasted_iota(jnp.int32, (wide, rows), 0) + (tile - 1) * cols
    inside = jnp.where(jnp.logical_and(x >= 0, x < n_tile * cols), F32(1.0), F32(0.0))
    total = n_sec * secs

    def prepare(s, carry):
        inv[s] = live[s, 0] + live[s, 1] + live[s, 2] + live[s, 3] + 1.0
        live[s, 2] = jnp.where(y > 0, live[s, 2], F32(0.0))
        live[s, 3] = jnp.where(y < rows - 1, live[s, 3], F32(0.0))
        return carry

    lax.fori_loop(1, 3 * secs - 1, prepare, 0)

    def gathered(now, s, c):
        d = disp[now, s, c]
        return (
            live[s, 0] * pltpu.roll(d, 1, 0)
            + live[s, 1] * pltpu.roll(d, wide - 1, 0)
            + live[s, 2] * pltpu.roll(d, 1, 1)
            + live[s, 3] * pltpu.roll(d, rows - 1, 1)
            + disp[now, s - 1, c]
            + disp[now, s + 1, c]
        )

    def gather_first(s, carry):
        for c in range(2):
            first[s, c] = gathered(0, s, c)
        return carry

    lax.fori_loop(1, 3 * secs - 1, gather_first, 0)

    wait_halo(3)
    spectrum(3)
    correlate(2)
    correlate(3)

    parts = []
    for parity in (0, 1):
        value = dot(col_tab[parity, :, pl.ds(0, HALF)], nyq[parity].astype(BF16))
        pair = pltpu.roll(value, SHIFTS - 1, 1)
        parts.append(cross_of(value[:HALF], value[HALF:], pair[:HALF], pair[HALF:]))
    for parity in (0, 1):
        cross[pl.ds(parity * HALF, HALF), pl.ds(0, SHIFTS)] = parts[parity][0]
        cross[pl.ds(PATCH + parity * HALF, HALF), pl.ds(0, SHIFTS)] = parts[parity][1]
    edge = dot(off_tab[pl.ds(0, SHIFTS)], cross[:, pl.ds(0, SHIFTS)]).astype(BF16).astype(F32)
    column = lax.broadcasted_iota(jnp.int32, (SHIFTS, SHIFTS), 1)
    sign = jnp.where(column % 2 == 0, F32(1.0), F32(-1.0))

    for s in range(secs):
        scale = (1.0 / float(PATCH) ** 4) / jnp.sqrt(
            energy[s:s + 1, :] * energy[s + 1:s + 2, :] + EPS)
        value = (maps[s] + edge[:, s:s + 1] * sign) * scale
        ncc_out[s, 0] = value
        upper = value.astype(BF16)
        lower = (value - upper.astype(F32)).astype(BF16)
        picked = dot(jnp.concatenate([upper, lower], axis=1), onehot[s])
        found = []
        for xi in range(cols):
            hit = place == offv[s, 0, xi:xi + 1, :]
            found.append(jnp.sum(
                jnp.where(hit, picked[:, xi * rows:(xi + 1) * rows], F32(0.0)),
                axis=0, keepdims=True))
        matched = jnp.concatenate(found, axis=0)
        wts[1, 1, s] = valid[s, 0].astype(F32) * (0.5 + 8.0 * (matched * matched))

    when(has_left, lambda: w_copy(0).start())
    when(has_right, lambda: w_copy(1).start())
    when(has_right, lambda: w_copy(0).wait_recv())
    when(has_left, lambda: w_copy(1).wait_recv())
    when(has_prev, lambda: w_copy(2).start())
    when(has_next, lambda: w_copy(3).start())
    when(has_prev, lambda: w_copy(3).wait_recv())
    when(has_next, lambda: w_copy(2).wait_recv())

    for at in range(1, 3 * secs - 1):
        w = jnp.concatenate([wts[at // secs, tb, at % secs] for tb in range(3)], axis=0)
        sid = sec * secs + (at - secs)
        one = jnp.where(jnp.logical_and(sid >= 0, sid < total), 1.0, 0.0)
        count = jnp.where(sid > 0, 1.0, 0.0) + jnp.where(sid < total - 1, 1.0, 0.0)
        share = inside * one / (inv[at] + count + w)
        inv[at] = share
        for c in range(2):
            push = w * disp[0, at, c]
            pull[at, c] = push
            disp[1, at, c] = (first[at, c] + push) * share

    now = 1
    for sweep in range(1, SWEEPS - 1):
        def relax(s, carry, now=now):
            for c in range(2):
                disp[1 - now, s, c] = (gathered(now, s, c) + pull[s, c]) * inv[s]
            return carry

        lax.fori_loop(1 + sweep, 3 * secs - 1 - sweep, relax, 0)
        now = 1 - now
    for s in range(secs):
        for c in range(2):
            at = secs + s
            value = (gathered(now, at, c) + pull[at, c]) * inv[at]
            disp_out[s, c] = value[cols:2 * cols]

    for s in range(secs):
        when(has_right, lambda: halo_copy(s, 1).wait_send())
        when(has_left, lambda: halo_copy(s, 0).wait_send())

    @pl.when(has_prev)
    def _():
        for part in range(3):
            next_copy(part).wait_send()

    for side in range(4):
        when(sides[side][0], lambda: ext_copy(side).wait_send())
        when(sides[side][0], lambda: w_copy(side).wait_send())


def shards(n_sec, n_tile, pixels, valid, offsets, neighbours):
    secs, _, cols, rows = offsets.shape
    width = pixels.shape[1]
    consts = [jnp.asarray(a) for a in tables()]
    ext_secs = 3 * secs
    any_space = pl.BlockSpec(memory_space=pl.ANY)
    vmem = pl.BlockSpec(memory_space=pltpu.VMEM)
    dma = pltpu.SemaphoreType.DMA
    return pl.pallas_call(
        functools.partial(kernel, n_sec, n_tile),
        out_shape=(
            jax.ShapeDtypeStruct((secs, 1, SHIFTS, SHIFTS), F32),
            jax.ShapeDtypeStruct((secs, 2, cols, rows), F32),
        ),
        in_specs=[any_space, pl.BlockSpec(memory_space=pltpu.SMEM)] + [any_space] * 6,
        out_specs=(vmem, vmem),
        scratch_shapes=[
            pltpu.VMEM((secs + 1, PATCH, PATCH), BF16),
            pltpu.VMEM(offsets.shape, jnp.int32),
            pltpu.VMEM(neighbours.shape, jnp.int32),
            pltpu.VMEM(consts[0].shape, BF16),
            pltpu.VMEM(consts[1].shape, BF16),
            pltpu.VMEM(consts[2].shape, BF16),
            pltpu.VMEM(consts[3].shape, BF16),
            pltpu.VMEM((secs + 1, width, PATCH), F32),
            pltpu.VMEM((2, PATCH, HALF), BF16),
            pltpu.VMEM((secs + 1, 2, PATCH, HALF), F32),
            pltpu.VMEM((2 * PATCH, HALF), BF16),
            pltpu.VMEM((2, HALF, SHIFTS), F32),
            pltpu.VMEM((secs, SHIFTS, SHIFTS), F32),
            pltpu.VMEM((8, SHIFTS), F32),
            pltpu.VMEM((secs, 2 * SHIFTS, cols * rows), BF16),
            pltpu.VMEM((3, 3, secs, 6 * cols, rows), BF16),
            pltpu.VMEM((3, 3, secs, cols, rows), F32),
            pltpu.VMEM((2, ext_secs, 2, 3 * cols, rows), F32),
            pltpu.VMEM((ext_secs, 4, 3 * cols, rows), F32),
            pltpu.VMEM((ext_secs, 3 * cols, rows), F32),
            pltpu.VMEM((ext_secs, 2, 3 * cols, rows), F32),
            pltpu.VMEM((ext_secs, 2, 3 * cols, rows), F32),
            dma((6 + secs,)),
            dma((secs, 2)), dma((secs, 2)),
            dma((3,)), dma((3,)),
            dma((4,)), dma((4,)),
            dma((4,)), dma((4,)),
        ],
        compiler_params=pltpu.CompilerParams(
            collective_id=0, has_side_effects=True, vmem_limit_bytes=48 * 2**20),
        name="align",
    )(pixels, valid, offsets, neighbours, *consts)


def solution(mesh):
    return jax.shard_map(
        functools.partial(shards, mesh.shape["sec"], mesh.shape["tile"]),
        mesh=mesh,
        in_specs=(
            P("sec", "tile", None),
            P("sec", "tile"),
            P("sec", None, "tile", None),
            P("sec", None, "tile", None),
        ),
        out_specs=(P("sec", "tile", None, None), P("sec", None, "tile", None)),
        check_vma=False,
    )
```

```python
import functools

import jax
import jax.numpy as jnp
import ml_dtypes
import numpy as np
from jax import lax
from jax.experimental import pallas as pl
from jax.experimental.pallas import tpu as pltpu
from jax.sharding import PartitionSpec as P

PATCH = 512
HALF = PATCH // 2
HALO = 128
SHIFTS = 128
SWEEPS = 4
EPS = 1e-06
F32 = jnp.float32
BF16 = jnp.bfloat16


def cos_sin(product):
    angles = (product % PATCH) * (2.0 * np.pi / PATCH)
    return np.cos(angles), np.sin(angles)


def tables():
    pos = np.arange(PATCH)
    freq = np.arange(HALF)
    cos, sin = cos_sin(pos[:, None] * freq[None, :])
    row_tab = np.concatenate([cos, -sin], axis=1)
    row_tab[:, HALF] = 1.0 - 2.0 * (pos % 2)
    col_tab = []
    for parity in (0, 1):
        cos, sin = cos_sin((2 * freq[:, None] + parity) * freq[None, :])
        col_tab.append(np.block([[cos, sin], [-sin, cos]]))
    shift = np.arange(SHIFTS) - SHIFTS // 2
    order = np.concatenate([2 * freq, 2 * freq + 1])
    cos, sin = cos_sin(shift[:, None] * order[None, :])
    off_tab = np.block([[cos, -sin], [sin, cos]])
    cos, sin = cos_sin(freq[:, None] * shift[None, :])
    twice = np.where(freq == 0, 1.0, 2.0)[:, None]
    map_tab = np.concatenate([cos * twice, -sin * twice], axis=0)
    return [
        np.asarray(a, np.float32).astype(ml_dtypes.bfloat16)
        for a in (row_tab, np.stack(col_tab), off_tab, map_tab)
    ]


def dot(a, b):
    return jnp.dot(a, b, preferred_element_type=F32)


def kernel(
    n_sec, n_tile,
    px, valid, off, nbr, row_hbm, col_hbm, offt_hbm, map_hbm,
    ncc_out, disp_out,
    win, offv, nbrv, row_tab, col_tab, off_tab, map_tab,
    own, mix, spec, cross, nyq, maps, energy, onehot,
    ext, wts, disp, live, inv, pull, first,
    loc_sem, halo_send, halo_recv, next_send, next_recv, ext_send, ext_recv, w_send, w_recv,
):
    sec = lax.axis_index("sec")
    tile = lax.axis_index("tile")
    secs = px.shape[0]
    width = px.shape[1]
    cols = off.shape[2]
    rows = off.shape[3]
    nxt = secs
    has_left, has_right = tile > 0, tile < n_tile - 1
    has_prev, has_next = sec > 0, sec < n_sec - 1
    sides = (
        (has_left, {"tile": tile - 1}),
        (has_right, {"tile": tile + 1}),
        (has_prev, {"sec": sec - 1}),
        (has_next, {"sec": sec + 1}),
    )

    def remote(src, dst, send, recv, to):
        return pltpu.make_async_remote_copy(
            src_ref=src, dst_ref=dst, send_sem=send, recv_sem=recv,
            device_id=to, device_id_type=pl.DeviceIdType.MESH,
        )

    barrier = pltpu.get_barrier_semaphore()
    for there, to in sides:
        @pl.when(there)
        def _(to=to):
            pl.semaphore_signal(barrier, inc=1, device_id=to, device_id_type=pl.DeviceIdType.MESH)

    local = [
        pltpu.make_async_copy(off, offv, loc_sem.at[0]),
        pltpu.make_async_copy(nbr, nbrv, loc_sem.at[1]),
        pltpu.make_async_copy(row_hbm, row_tab, loc_sem.at[2]),
        pltpu.make_async_copy(col_hbm, col_tab, loc_sem.at[3]),
        pltpu.make_async_copy(offt_hbm, off_tab, loc_sem.at[4]),
        pltpu.make_async_copy(map_hbm, map_tab, loc_sem.at[5]),
    ]
    mine = [
        pltpu.make_async_copy(px.at[s], win.at[s, pl.ds(HALO, width)], loc_sem.at[6 + s])
        for s in range(secs)
    ]
    pl.semaphore_wait(barrier, sum(there.astype(jnp.int32) for there, _ in sides))

    low = pl.ds(0, HALO)
    high = pl.ds(HALO + width, HALO)

    def halo_copy(s, side):
        if side == 0:
            return remote(px.at[s, pl.ds(0, HALO)], win.at[s, high],
                          halo_send.at[s, 0], halo_recv.at[s, 1], sides[0][1])
        return remote(px.at[s, pl.ds(width - HALO, HALO)], win.at[s, low],
                      halo_send.at[s, 1], halo_recv.at[s, 0], sides[1][1])

    def next_copy(part):
        if part == 0:
            src, dst = px.at[0], win.at[nxt, pl.ds(HALO, width)]
        else:
            place = low if part == 1 else high
            src, dst = win.at[0, place], win.at[nxt, place]
        return remote(src, dst, next_send.at[part], next_recv.at[part], sides[2][1])

    def ext_copy(side):
        if side < 2:
            src, dst = ext.at[1, 1], ext.at[1, 2 - 2 * side]
        else:
            src, dst = ext.at[1], ext.at[2 - 2 * (side - 2)]
        return remote(src, dst, ext_send.at[side], ext_recv.at[side ^ 1], sides[side][1])

    def w_copy(side):
        if side < 2:
            src, dst = wts.at[1, 1], wts.at[1, 2 - 2 * side]
        else:
            src, dst = wts.at[1], wts.at[2 - 2 * (side - 2)]
        return remote(src, dst, w_send.at[side], w_recv.at[side ^ 1], sides[side][1])

    def when(there, action):
        pl.when(there)(action)

    def send_halo(s):
        when(has_right, lambda: halo_copy(s, 1).start())
        when(has_left, lambda: halo_copy(s, 0).start())

    send_halo(0)
    send_halo(1)
    when(has_prev, lambda: next_copy(0).start())
    for copy in local + mine:
        copy.start()

    @pl.when(jnp.logical_not(has_left))
    def _():
        for s in range(secs):
            win[s, low] = jnp.zeros((HALO, PATCH), BF16)
        ext[1, 0] = jnp.zeros(ext.shape[2:], BF16)
        wts[1, 0] = jnp.zeros(wts.shape[2:], F32)

    @pl.when(jnp.logical_not(has_right))
    def _():
        for s in range(secs):
            win[s, high] = jnp.zeros((HALO, PATCH), BF16)
        ext[1, 2] = jnp.zeros(ext.shape[2:], BF16)
        wts[1, 2] = jnp.zeros(wts.shape[2:], F32)

    @pl.when(jnp.logical_not(has_prev))
    def _():
        ext[0] = jnp.zeros(ext.shape[1:], BF16)
        wts[0] = jnp.zeros(wts.shape[1:], F32)

    @pl.when(jnp.logical_not(has_next))
    def _():
        win[nxt] = jnp.zeros((PATCH, PATCH), BF16)
        ext[2] = jnp.zeros(ext.shape[1:], BF16)
        wts[2] = jnp.zeros(wts.shape[1:], F32)

    nyq[...] = jnp.zeros(nyq.shape, F32)

    local[0].wait()
    local[1].wait()
    limit = (cols + 2) * rows
    for s in range(secs):
        ext[1, 1, s, pl.ds(0, 2 * cols)] = offv[s].reshape(2 * cols, rows).astype(F32).astype(BF16)
        ext[1, 1, s, pl.ds(2 * cols, 4 * cols)] = jnp.where(
            nbrv[s].reshape(4 * cols, rows) < limit, F32(1.0), F32(0.0)).astype(BF16)
    when(has_left, lambda: ext_copy(0).start())
    when(has_right, lambda: ext_copy(1).start())

    local[2].wait()

    def own_rows(j):
        own[j] = dot(win[j, pl.ds(HALO, width)], row_tab[...])

    for s in range(secs):
        mine[s].wait()
        own_rows(s)

    half_win = SHIFTS // 2
    place = lax.broadcasted_iota(jnp.int32, (SHIFTS, rows), 0) - half_win

    def fill_onehot(s):
        for x in range(cols):
            hit = jnp.where(place == offv[s, 1, x:x + 1, :], F32(1.0), F32(0.0)).astype(BF16)
            onehot[s, pl.ds(0, SHIFTS), pl.ds(x * rows, rows)] = hit
            onehot[s, pl.ds(SHIFTS, SHIFTS), pl.ds(x * rows, rows)] = hit

    for s in range(secs):
        fill_onehot(s)
    for copy in local[3:]:
        copy.wait()

    lane = lax.broadcasted_iota(jnp.int32, (HALO, SHIFTS), 1)
    lane_wide = lax.broadcasted_iota(jnp.int32, (HALO, HALF), 1)

    def spectrum(j):
        pix = win[j].astype(F32)
        total = jnp.sum(jnp.sum(pix * pix, axis=0, keepdims=True), axis=1, keepdims=True)
        energy[j:j + 1, :] = jnp.broadcast_to(total * (1.0 / (PATCH * PATCH)), (1, SHIFTS))
        first_rows = dot(win[j, low], row_tab[...])
        last_rows = dot(win[j, high], row_tab[...])
        for part, (a, b) in enumerate((
            (first_rows, own[j, pl.ds(HALO, HALO)]),
            (own[j, pl.ds(0, HALO)], last_rows),
        )):
            for parity, value in enumerate((a + b, a - b)):
                mix[parity, pl.ds(part * HALO, HALO)] = value[:, :HALF].astype(BF16)
                mix[parity, pl.ds(HALF + part * HALO, HALO)] = jnp.where(
                    lane_wide == 0, F32(0.0), value[:, HALF:]).astype(BF16)
                at = (parity, pl.ds(part * HALO, HALO))
                nyq[at] = jnp.where(lane == j, value[:, HALF:HALF + 1], nyq[at])
        for parity in (0, 1):
            spec[j, parity] = dot(col_tab[parity], mix[parity])

    def cross_of(p_re, p_im, q_re, q_im):
        return (
            (p_re * q_re + p_im * q_im).astype(BF16),
            (p_re * q_im - p_im * q_re).astype(BF16),
        )

    def correlate(s):
        for parity in (0, 1):
            re, im = cross_of(
                spec[s, parity, pl.ds(0, HALF)], spec[s, parity, pl.ds(HALF, HALF)],
                spec[s + 1, parity, pl.ds(0, HALF)], spec[s + 1, parity, pl.ds(HALF, HALF)])
            cross[pl.ds(parity * HALF, HALF)] = re
            cross[pl.ds(PATCH + parity * HALF, HALF)] = im
        half = dot(off_tab[...], cross[...]).astype(BF16)
        maps[s] = dot(half[:SHIFTS], map_tab[pl.ds(0, HALF)]) + dot(
            half[SHIFTS:], map_tab[pl.ds(HALF, HALF)])

    column = lax.broadcasted_iota(jnp.int32, (SHIFTS, SHIFTS), 1)
    sign = jnp.where(column % 2 == 0, F32(1.0), F32(-1.0))

    def finish(some):
        parts = []
        for parity in (0, 1):
            value = dot(col_tab[parity, :, pl.ds(0, HALF)], nyq[parity].astype(BF16))
            pair = pltpu.roll(value, SHIFTS - 1, 1)
            parts.append(cross_of(value[:HALF], value[HALF:], pair[:HALF], pair[HALF:]))
        both = jnp.concatenate([parts[0][0], parts[1][0], parts[0][1], parts[1][1]], axis=0)
        edge = dot(off_tab[pl.ds(0, SHIFTS)], both).astype(BF16).astype(F32)
        for s in some:
            scale = (1.0 / float(PATCH) ** 4) / jnp.sqrt(
                energy[s:s + 1, :] * energy[s + 1:s + 2, :] + EPS)
            value = (maps[s] + edge[:, s:s + 1] * sign) * scale
            ncc_out[s, 0] = value
            upper = value.astype(BF16)
            lower = (value - upper.astype(F32)).astype(BF16)
            picked = dot(jnp.concatenate([upper, lower], axis=1), onehot[s])
            found = []
            for xi in range(cols):
                hit = place == offv[s, 0, xi:xi + 1, :]
                found.append(jnp.sum(
                    jnp.where(hit, picked[:, xi * rows:(xi + 1) * rows], F32(0.0)),
                    axis=0, keepdims=True))
            matched = jnp.concatenate(found, axis=0)
            wts[1, 1, s] = valid[0, s].astype(F32) * (0.5 + 8.0 * (matched * matched))

    def wait_halo(s):
        when(has_left, lambda: halo_copy(s, 1).wait_recv())
        when(has_right, lambda: halo_copy(s, 0).wait_recv())

    wait_halo(0)
    send_halo(2)

    @pl.when(has_prev)
    def _():
        next_copy(1).start()
        next_copy(2).start()

    spectrum(0)
    when(has_right, lambda: ext_copy(0).wait_recv())
    when(has_left, lambda: ext_copy(1).wait_recv())
    when(has_prev, lambda: ext_copy(2).start())
    when(has_next, lambda: ext_copy(3).start())
    wait_halo(1)
    send_halo(3)
    spectrum(1)
    correlate(0)

    @pl.when(has_next)
    def _():
        for part in range(3):
            next_copy(part).wait_recv()

    own_rows(nxt)
    spectrum(nxt)
    wait_halo(2)
    spectrum(2)
    correlate(1)
    finish(range(secs - 2))

    when(has_prev, lambda: ext_copy(3).wait_recv())
    when(has_next, lambda: ext_copy(2).wait_recv())
    wide = 3 * cols
    for sb in range(3):
        for s in range(secs):
            at = sb * secs + s
            for tb in range(3):
                for c in range(2):
                    disp[0, at, c, pl.ds(tb * cols, cols)] = ext[
                        sb, tb, s, pl.ds(0, 2 * cols)].astype(F32)[
                            c * cols:(c + 1) * cols] * (2.0 / SHIFTS)
                for d in range(4):
                    live[at, d, pl.ds(tb * cols, cols)] = ext[
                        sb, tb, s, pl.ds(2 * cols, 4 * cols)].astype(F32)[d * cols:(d + 1) * cols]
    y = lax.broadcasted_iota(jnp.int32, (wide, rows), 1)
    x = lax.broadcasted_iota(jnp.int32, (wide, rows), 0) + (tile - 1) * cols
    inside = jnp.where(jnp.logical_and(x >= 0, x < n_tile * cols), F32(1.0), F32(0.0))
    total = n_sec * secs

    def prepare(s, carry):
        inv[s] = live[s, 0] + live[s, 1] + live[s, 2] + live[s, 3] + 1.0
        live[s, 2] = jnp.where(y > 0, live[s, 2], F32(0.0))
        live[s, 3] = jnp.where(y < rows - 1, live[s, 3], F32(0.0))
        return carry

    lax.fori_loop(1, 3 * secs - 1, prepare, 0)

    def gathered(now, s, c):
        d = disp[now, s, c]
        return (
            live[s, 0] * pltpu.roll(d, 1, 0)
            + live[s, 1] * pltpu.roll(d, wide - 1, 0)
            + live[s, 2] * pltpu.roll(d, 1, 1)
            + live[s, 3] * pltpu.roll(d, rows - 1, 1)
            + disp[now, s - 1, c]
            + disp[now, s + 1, c]
        )

    def gather_first(s, carry):
        for c in range(2):
            first[s, c] = gathered(0, s, c)
        return carry

    lax.fori_loop(1, 3 * secs - 1, gather_first, 0)

    wait_halo(3)
    spectrum(3)
    correlate(2)
    correlate(3)

    finish(range(secs - 2, secs))

    when(has_left, lambda: w_copy(0).start())
    when(has_right, lambda: w_copy(1).start())
    when(has_right, lambda: w_copy(0).wait_recv())
    when(has_left, lambda: w_copy(1).wait_recv())
    when(has_prev, lambda: w_copy(2).start())
    when(has_next, lambda: w_copy(3).start())
    when(has_prev, lambda: w_copy(3).wait_recv())
    when(has_next, lambda: w_copy(2).wait_recv())

    for at in range(1, 3 * secs - 1):
        w = jnp.concatenate([wts[at // secs, tb, at % secs] for tb in range(3)], axis=0)
        sid = sec * secs + (at - secs)
        one = jnp.where(jnp.logical_and(sid >= 0, sid < total), 1.0, 0.0)
        count = jnp.where(sid > 0, 1.0, 0.0) + jnp.where(sid < total - 1, 1.0, 0.0)
        share = inside * one / (inv[at] + count + w)
        inv[at] = share
        for c in range(2):
            push = w * disp[0, at, c]
            pull[at, c] = push
            disp[1, at, c] = (first[at, c] + push) * share

    now = 1
    for sweep in range(1, SWEEPS - 1):
        def relax(s, carry, now=now):
            for c in range(2):
                disp[1 - now, s, c] = (gathered(now, s, c) + pull[s, c]) * inv[s]
            return carry

        lax.fori_loop(1 + sweep, 3 * secs - 1 - sweep, relax, 0)
        now = 1 - now
    for s in range(secs):
        for c in range(2):
            at = secs + s
            value = (gathered(now, at, c) + pull[at, c]) * inv[at]
            disp_out[s, c] = value[cols:2 * cols]

    for s in range(secs):
        when(has_right, lambda: halo_copy(s, 1).wait_send())
        when(has_left, lambda: halo_copy(s, 0).wait_send())

    @pl.when(has_prev)
    def _():
        for part in range(3):
            next_copy(part).wait_send()

    for side in range(4):
        when(sides[side][0], lambda: ext_copy(side).wait_send())
        when(sides[side][0], lambda: w_copy(side).wait_send())


def shards(n_sec, n_tile, pixels, valid, offsets, neighbours):
    secs, _, cols, rows = offsets.shape
    width = pixels.shape[1]
    consts = [jnp.asarray(a) for a in tables()]
    ext_secs = 3 * secs
    hbm = pl.BlockSpec(memory_space=pltpu.HBM)
    vmem = pl.BlockSpec(memory_space=pltpu.VMEM)
    dma = pltpu.SemaphoreType.DMA
    return pl.pallas_call(
        functools.partial(kernel, n_sec, n_tile),
        out_shape=(
            jax.ShapeDtypeStruct((secs, 1, SHIFTS, SHIFTS), F32),
            jax.ShapeDtypeStruct((secs, 2, cols, rows), F32),
        ),
        in_specs=[hbm, pl.BlockSpec(memory_space=pltpu.SMEM)] + [hbm] * 6,
        out_specs=(vmem, vmem),
        scratch_shapes=[
            pltpu.VMEM((secs + 1, PATCH, PATCH), BF16),
            pltpu.VMEM(offsets.shape, jnp.int32),
            pltpu.VMEM(neighbours.shape, jnp.int32),
            pltpu.VMEM(consts[0].shape, BF16),
            pltpu.VMEM(consts[1].shape, BF16),
            pltpu.VMEM(consts[2].shape, BF16),
            pltpu.VMEM(consts[3].shape, BF16),
            pltpu.VMEM((secs + 1, width, PATCH), F32),
            pltpu.VMEM((2, PATCH, HALF), BF16),
            pltpu.VMEM((secs + 1, 2, PATCH, HALF), F32),
            pltpu.VMEM((2 * PATCH, HALF), BF16),
            pltpu.VMEM((2, HALF, SHIFTS), F32),
            pltpu.VMEM((secs, SHIFTS, SHIFTS), F32),
            pltpu.VMEM((8, SHIFTS), F32),
            pltpu.VMEM((secs, 2 * SHIFTS, cols * rows), BF16),
            pltpu.VMEM((3, 3, secs, 6 * cols, rows), BF16),
            pltpu.VMEM((3, 3, secs, cols, rows), F32),
            pltpu.VMEM((2, ext_secs, 2, 3 * cols, rows), F32),
            pltpu.VMEM((ext_secs, 4, 3 * cols, rows), F32),
            pltpu.VMEM((ext_secs, 3 * cols, rows), F32),
            pltpu.VMEM((ext_secs, 2, 3 * cols, rows), F32),
            pltpu.VMEM((ext_secs, 2, 3 * cols, rows), F32),
            dma((6 + secs,)),
            dma((secs, 2)), dma((secs, 2)),
            dma((3,)), dma((3,)),
            dma((4,)), dma((4,)),
            dma((4,)), dma((4,)),
        ],
        compiler_params=pltpu.CompilerParams(
            collective_id=0, has_side_effects=True, vmem_limit_bytes=63 * 2**20),
        name="align",
    )(pixels, valid.reshape(1, secs), offsets, neighbours, *consts)


def solution(mesh):
    return jax.shard_map(
        functools.partial(shards, mesh.shape["sec"], mesh.shape["tile"]),
        mesh=mesh,
        in_specs=(
            P("sec", "tile", None),
            P("sec", "tile"),
            P("sec", None, "tile", None),
            P("sec", None, "tile", None),
        ),
        out_specs=(P("sec", "tile", None, None), P("sec", None, "tile", None)),
        check_vma=False,
    )
```

```python
import functools

import jax
import jax.numpy as jnp
import ml_dtypes
import numpy as np
from jax import lax
from jax.experimental import pallas as pl
from jax.experimental.pallas import tpu as pltpu
from jax.sharding import PartitionSpec as P

PATCH = 512
HALF = PATCH // 2
HALO = 128
SHIFTS = 128
SWEEPS = 4
EPS = 1e-06
F32 = jnp.float32
BF16 = jnp.bfloat16


def cos_sin(product):
    angles = (product % PATCH) * (2.0 * np.pi / PATCH)
    return np.cos(angles), np.sin(angles)


def tables():
    pos = np.arange(PATCH)
    freq = np.arange(HALF)
    cos, sin = cos_sin(pos[:, None] * freq[None, :])
    row_tab = np.concatenate([cos, -sin], axis=1)
    row_tab[:, HALF] = 1.0 - 2.0 * (pos % 2)
    col_tab = []
    for parity in (0, 1):
        cos, sin = cos_sin((2 * freq[:, None] + parity) * freq[None, :])
        col_tab.append(np.block([[cos, sin], [-sin, cos]]))
    shift = np.arange(SHIFTS) - SHIFTS // 2
    order = np.concatenate([2 * freq, 2 * freq + 1])
    cos, sin = cos_sin(shift[:, None] * order[None, :])
    off_tab = np.block([[cos, -sin], [sin, cos]])
    cos, sin = cos_sin(freq[:, None] * shift[None, :])
    twice = np.where(freq == 0, 1.0, 2.0)[:, None]
    map_tab = np.concatenate([cos * twice, -sin * twice], axis=0)
    return [
        np.asarray(a, np.float32).astype(ml_dtypes.bfloat16)
        for a in (row_tab, np.stack(col_tab), off_tab, map_tab)
    ]


def dot(a, b):
    return jnp.dot(a, b, preferred_element_type=F32)


def kernel(
    n_sec, n_tile,
    px, valid, off, nbr, row_hbm, col_hbm, offt_hbm, map_hbm,
    ncc_out, disp_out,
    win, offv, nbrv, row_tab, col_tab, off_tab, map_tab,
    own, mix, spec, cross, nyq, maps, energy, onehot,
    ext, wts, disp, live, inv, pull, first,
    loc_sem, halo_send, halo_recv, next_send, next_recv, ext_send, ext_recv, w_send, w_recv,
):
    sec = lax.axis_index("sec")
    tile = lax.axis_index("tile")
    secs = px.shape[0]
    width = px.shape[1]
    cols = off.shape[2]
    rows = off.shape[3]
    nxt = secs
    has_left, has_right = tile > 0, tile < n_tile - 1
    has_prev, has_next = sec > 0, sec < n_sec - 1
    sides = (
        (has_left, {"tile": tile - 1}),
        (has_right, {"tile": tile + 1}),
        (has_prev, {"sec": sec - 1}),
        (has_next, {"sec": sec + 1}),
    )

    def remote(src, dst, send, recv, to):
        return pltpu.make_async_remote_copy(
            src_ref=src, dst_ref=dst, send_sem=send, recv_sem=recv,
            device_id=to, device_id_type=pl.DeviceIdType.MESH,
        )

    barrier = pltpu.get_barrier_semaphore()
    for there, to in sides:
        @pl.when(there)
        def _(to=to):
            pl.semaphore_signal(barrier, inc=1, device_id=to, device_id_type=pl.DeviceIdType.MESH)

    local = [
        pltpu.make_async_copy(off, offv, loc_sem.at[0]),
        pltpu.make_async_copy(nbr, nbrv, loc_sem.at[1]),
        pltpu.make_async_copy(row_hbm, row_tab, loc_sem.at[2]),
        pltpu.make_async_copy(col_hbm, col_tab, loc_sem.at[3]),
        pltpu.make_async_copy(offt_hbm, off_tab, loc_sem.at[4]),
        pltpu.make_async_copy(map_hbm, map_tab, loc_sem.at[5]),
    ]
    mine = [
        pltpu.make_async_copy(px.at[s], win.at[s, pl.ds(HALO, width)], loc_sem.at[6 + s])
        for s in range(secs)
    ]
    pl.semaphore_wait(barrier, sum(there.astype(jnp.int32) for there, _ in sides))

    low = pl.ds(0, HALO)
    high = pl.ds(HALO + width, HALO)

    def halo_copy(s, side):
        if side == 0:
            return remote(px.at[s, pl.ds(0, HALO)], win.at[s, high],
                          halo_send.at[s, 0], halo_recv.at[s, 1], sides[0][1])
        return remote(px.at[s, pl.ds(width - HALO, HALO)], win.at[s, low],
                      halo_send.at[s, 1], halo_recv.at[s, 0], sides[1][1])

    def next_copy(part):
        if part == 0:
            src, dst = px.at[0], win.at[nxt, pl.ds(HALO, width)]
        else:
            place = low if part == 1 else high
            src, dst = win.at[0, place], win.at[nxt, place]
        return remote(src, dst, next_send.at[part], next_recv.at[part], sides[2][1])

    def ext_copy(side):
        if side < 2:
            src, dst = ext.at[1, 1], ext.at[1, 2 - 2 * side]
        else:
            src, dst = ext.at[1], ext.at[2 - 2 * (side - 2)]
        return remote(src, dst, ext_send.at[side], ext_recv.at[side ^ 1], sides[side][1])

    def w_copy(side):
        if side < 2:
            src, dst = wts.at[1, 1], wts.at[1, 2 - 2 * side]
        else:
            src, dst = wts.at[1], wts.at[2 - 2 * (side - 2)]
        return remote(src, dst, w_send.at[side], w_recv.at[side ^ 1], sides[side][1])

    def when(there, action):
        pl.when(there)(action)

    def send_halo(s):
        when(has_right, lambda: halo_copy(s, 1).start())
        when(has_left, lambda: halo_copy(s, 0).start())

    send_halo(0)
    send_halo(1)
    when(has_prev, lambda: next_copy(0).start())
    for copy in local + mine:
        copy.start()

    @pl.when(jnp.logical_not(has_left))
    def _():
        for s in range(secs):
            win[s, low] = jnp.zeros((HALO, PATCH), BF16)
        ext[1, 0] = jnp.zeros(ext.shape[2:], BF16)
        wts[1, 0] = jnp.zeros(wts.shape[2:], F32)

    @pl.when(jnp.logical_not(has_right))
    def _():
        for s in range(secs):
            win[s, high] = jnp.zeros((HALO, PATCH), BF16)
        ext[1, 2] = jnp.zeros(ext.shape[2:], BF16)
        wts[1, 2] = jnp.zeros(wts.shape[2:], F32)

    @pl.when(jnp.logical_not(has_prev))
    def _():
        ext[0] = jnp.zeros(ext.shape[1:], BF16)
        wts[0] = jnp.zeros(wts.shape[1:], F32)

    @pl.when(jnp.logical_not(has_next))
    def _():
        win[nxt] = jnp.zeros((PATCH, PATCH), BF16)
        ext[2] = jnp.zeros(ext.shape[1:], BF16)
        wts[2] = jnp.zeros(wts.shape[1:], F32)

    nyq[...] = jnp.zeros(nyq.shape, F32)

    local[0].wait()
    local[1].wait()
    limit = (cols + 2) * rows
    for s in range(secs):
        ext[1, 1, s, pl.ds(0, 2 * cols)] = offv[s].reshape(2 * cols, rows).astype(F32).astype(BF16)
        ext[1, 1, s, pl.ds(2 * cols, 4 * cols)] = jnp.where(
            nbrv[s].reshape(4 * cols, rows) < limit, F32(1.0), F32(0.0)).astype(BF16)

    local[2].wait()

    def own_rows(j):
        own[j] = dot(win[j, pl.ds(HALO, width)], row_tab[...])

    for s in range(secs):
        mine[s].wait()
        own_rows(s)

    half_win = SHIFTS // 2
    place = lax.broadcasted_iota(jnp.int32, (SHIFTS, rows), 0) - half_win

    def fill_onehot(s):
        for x in range(cols):
            hit = jnp.where(place == offv[s, 1, x:x + 1, :], F32(1.0), F32(0.0)).astype(BF16)
            onehot[s, pl.ds(0, SHIFTS), pl.ds(x * rows, rows)] = hit
            onehot[s, pl.ds(SHIFTS, SHIFTS), pl.ds(x * rows, rows)] = hit

    for s in range(secs):
        fill_onehot(s)
    for copy in local[3:]:
        copy.wait()

    lane = lax.broadcasted_iota(jnp.int32, (HALO, SHIFTS), 1)
    lane_wide = lax.broadcasted_iota(jnp.int32, (HALO, HALF), 1)

    def spectrum(j):
        pix = win[j].astype(F32)
        total = jnp.sum(jnp.sum(pix * pix, axis=0, keepdims=True), axis=1, keepdims=True)
        energy[j:j + 1, :] = jnp.broadcast_to(total * (1.0 / (PATCH * PATCH)), (1, SHIFTS))
        first_rows = dot(win[j, low], row_tab[...])
        last_rows = dot(win[j, high], row_tab[...])
        for part, (a, b) in enumerate((
            (first_rows, own[j, pl.ds(HALO, HALO)]),
            (own[j, pl.ds(0, HALO)], last_rows),
        )):
            for parity, value in enumerate((a + b, a - b)):
                mix[parity, pl.ds(part * HALO, HALO)] = value[:, :HALF].astype(BF16)
                mix[parity, pl.ds(HALF + part * HALO, HALO)] = jnp.where(
                    lane_wide == 0, F32(0.0), value[:, HALF:]).astype(BF16)
                at = (parity, pl.ds(part * HALO, HALO))
                nyq[at] = jnp.where(lane == j, value[:, HALF:HALF + 1], nyq[at])
        for parity in (0, 1):
            spec[j, parity] = dot(col_tab[parity], mix[parity])

    def cross_of(p_re, p_im, q_re, q_im):
        return (
            (p_re * q_re + p_im * q_im).astype(BF16),
            (p_re * q_im - p_im * q_re).astype(BF16),
        )

    def correlate(s):
        for parity in (0, 1):
            re, im = cross_of(
                spec[s, parity, pl.ds(0, HALF)], spec[s, parity, pl.ds(HALF, HALF)],
                spec[s + 1, parity, pl.ds(0, HALF)], spec[s + 1, parity, pl.ds(HALF, HALF)])
            cross[pl.ds(parity * HALF, HALF)] = re
            cross[pl.ds(PATCH + parity * HALF, HALF)] = im
        half = dot(off_tab[...], cross[...]).astype(BF16)
        maps[s] = dot(half[:SHIFTS], map_tab[pl.ds(0, HALF)]) + dot(
            half[SHIFTS:], map_tab[pl.ds(HALF, HALF)])

    column = lax.broadcasted_iota(jnp.int32, (SHIFTS, SHIFTS), 1)
    sign = jnp.where(column % 2 == 0, F32(1.0), F32(-1.0))

    def finish(some):
        parts = []
        for parity in (0, 1):
            value = dot(col_tab[parity, :, pl.ds(0, HALF)], nyq[parity].astype(BF16))
            pair = pltpu.roll(value, SHIFTS - 1, 1)
            parts.append(cross_of(value[:HALF], value[HALF:], pair[:HALF], pair[HALF:]))
        both = jnp.concatenate([parts[0][0], parts[1][0], parts[0][1], parts[1][1]], axis=0)
        edge = dot(off_tab[pl.ds(0, SHIFTS)], both).astype(BF16).astype(F32)
        for s in some:
            scale = (1.0 / float(PATCH) ** 4) / jnp.sqrt(
                energy[s:s + 1, :] * energy[s + 1:s + 2, :] + EPS)
            value = (maps[s] + edge[:, s:s + 1] * sign) * scale
            ncc_out[s, 0] = value
            upper = value.astype(BF16)
            lower = (value - upper.astype(F32)).astype(BF16)
            picked = dot(jnp.concatenate([upper, lower], axis=1), onehot[s])
            found = []
            for xi in range(cols):
                hit = place == offv[s, 0, xi:xi + 1, :]
                found.append(jnp.sum(
                    jnp.where(hit, picked[:, xi * rows:(xi + 1) * rows], F32(0.0)),
                    axis=0, keepdims=True))
            matched = jnp.concatenate(found, axis=0)
            wts[1, 1, s] = valid[0, s].astype(F32) * (0.5 + 8.0 * (matched * matched))

    def wait_halo(s):
        when(has_left, lambda: halo_copy(s, 1).wait_recv())
        when(has_right, lambda: halo_copy(s, 0).wait_recv())

    wait_halo(0)
    send_halo(2)
    when(has_left, lambda: ext_copy(0).start())
    when(has_right, lambda: ext_copy(1).start())

    @pl.when(has_prev)
    def _():
        next_copy(1).start()
        next_copy(2).start()

    spectrum(0)
    wait_halo(1)
    send_halo(3)
    spectrum(1)
    correlate(0)
    when(has_right, lambda: ext_copy(0).wait_recv())
    when(has_left, lambda: ext_copy(1).wait_recv())
    when(has_prev, lambda: ext_copy(2).start())
    when(has_next, lambda: ext_copy(3).start())

    @pl.when(has_next)
    def _():
        for part in range(3):
            next_copy(part).wait_recv()

    own_rows(nxt)
    spectrum(nxt)
    wait_halo(2)
    spectrum(2)
    correlate(1)
    finish(range(secs - 2))

    when(has_prev, lambda: ext_copy(3).wait_recv())
    when(has_next, lambda: ext_copy(2).wait_recv())
    wide = 3 * cols
    for sb in range(3):
        for s in range(secs):
            at = sb * secs + s
            for tb in range(3):
                for c in range(2):
                    disp[0, at, c, pl.ds(tb * cols, cols)] = ext[
                        sb, tb, s, pl.ds(0, 2 * cols)].astype(F32)[
                            c * cols:(c + 1) * cols] * (2.0 / SHIFTS)
                for d in range(4):
                    live[at, d, pl.ds(tb * cols, cols)] = ext[
                        sb, tb, s, pl.ds(2 * cols, 4 * cols)].astype(F32)[d * cols:(d + 1) * cols]
    y = lax.broadcasted_iota(jnp.int32, (wide, rows), 1)
    x = lax.broadcasted_iota(jnp.int32, (wide, rows), 0) + (tile - 1) * cols
    inside = jnp.where(jnp.logical_and(x >= 0, x < n_tile * cols), F32(1.0), F32(0.0))
    total = n_sec * secs

    def prepare(s, carry):
        inv[s] = live[s, 0] + live[s, 1] + live[s, 2] + live[s, 3] + 1.0
        live[s, 2] = jnp.where(y > 0, live[s, 2], F32(0.0))
        live[s, 3] = jnp.where(y < rows - 1, live[s, 3], F32(0.0))
        return carry

    lax.fori_loop(1, 3 * secs - 1, prepare, 0)

    def gathered(now, s, c):
        d = disp[now, s, c]
        return (
            live[s, 0] * pltpu.roll(d, 1, 0)
            + live[s, 1] * pltpu.roll(d, wide - 1, 0)
            + live[s, 2] * pltpu.roll(d, 1, 1)
            + live[s, 3] * pltpu.roll(d, rows - 1, 1)
            + disp[now, s - 1, c]
            + disp[now, s + 1, c]
        )

    def gather_first(s, carry):
        for c in range(2):
            first[s, c] = gathered(0, s, c)
        return carry

    lax.fori_loop(1, 3 * secs - 1, gather_first, 0)

    wait_halo(3)
    spectrum(3)
    correlate(2)
    correlate(3)

    finish(range(secs - 2, secs))

    when(has_left, lambda: w_copy(0).start())
    when(has_right, lambda: w_copy(1).start())
    when(has_right, lambda: w_copy(0).wait_recv())
    when(has_left, lambda: w_copy(1).wait_recv())
    when(has_prev, lambda: w_copy(2).start())
    when(has_next, lambda: w_copy(3).start())
    when(has_prev, lambda: w_copy(3).wait_recv())
    when(has_next, lambda: w_copy(2).wait_recv())

    for at in range(1, 3 * secs - 1):
        w = jnp.concatenate([wts[at // secs, tb, at % secs] for tb in range(3)], axis=0)
        sid = sec * secs + (at - secs)
        one = jnp.where(jnp.logical_and(sid >= 0, sid < total), 1.0, 0.0)
        count = jnp.where(sid > 0, 1.0, 0.0) + jnp.where(sid < total - 1, 1.0, 0.0)
        share = inside * one / (inv[at] + count + w)
        inv[at] = share
        for c in range(2):
            push = w * disp[0, at, c]
            pull[at, c] = push
            disp[1, at, c] = (first[at, c] + push) * share

    now = 1
    for sweep in range(1, SWEEPS - 1):
        def relax(s, carry, now=now):
            for c in range(2):
                disp[1 - now, s, c] = (gathered(now, s, c) + pull[s, c]) * inv[s]
            return carry

        lax.fori_loop(1 + sweep, 3 * secs - 1 - sweep, relax, 0)
        now = 1 - now
    for s in range(secs):
        for c in range(2):
            at = secs + s
            value = (gathered(now, at, c) + pull[at, c]) * inv[at]
            disp_out[s, c] = value[cols:2 * cols]

    for s in range(secs):
        when(has_right, lambda: halo_copy(s, 1).wait_send())
        when(has_left, lambda: halo_copy(s, 0).wait_send())

    @pl.when(has_prev)
    def _():
        for part in range(3):
            next_copy(part).wait_send()

    for side in range(4):
        when(sides[side][0], lambda: ext_copy(side).wait_send())
        when(sides[side][0], lambda: w_copy(side).wait_send())


def shards(n_sec, n_tile, pixels, valid, offsets, neighbours):
    secs, _, cols, rows = offsets.shape
    width = pixels.shape[1]
    consts = [jnp.asarray(a) for a in tables()]
    ext_secs = 3 * secs
    hbm = pl.BlockSpec(memory_space=pltpu.HBM)
    vmem = pl.BlockSpec(memory_space=pltpu.VMEM)
    dma = pltpu.SemaphoreType.DMA
    return pl.pallas_call(
        functools.partial(kernel, n_sec, n_tile),
        out_shape=(
            jax.ShapeDtypeStruct((secs, 1, SHIFTS, SHIFTS), F32),
            jax.ShapeDtypeStruct((secs, 2, cols, rows), F32),
        ),
        in_specs=[hbm, pl.BlockSpec(memory_space=pltpu.SMEM)] + [hbm] * 6,
        out_specs=(vmem, vmem),
        scratch_shapes=[
            pltpu.VMEM((secs + 1, PATCH, PATCH), BF16),
            pltpu.VMEM(offsets.shape, jnp.int32),
            pltpu.VMEM(neighbours.shape, jnp.int32),
            pltpu.VMEM(consts[0].shape, BF16),
            pltpu.VMEM(consts[1].shape, BF16),
            pltpu.VMEM(consts[2].shape, BF16),
            pltpu.VMEM(consts[3].shape, BF16),
            pltpu.VMEM((secs + 1, width, PATCH), F32),
            pltpu.VMEM((2, PATCH, HALF), BF16),
            pltpu.VMEM((secs + 1, 2, PATCH, HALF), F32),
            pltpu.VMEM((2 * PATCH, HALF), BF16),
            pltpu.VMEM((2, HALF, SHIFTS), F32),
            pltpu.VMEM((secs, SHIFTS, SHIFTS), F32),
            pltpu.VMEM((8, SHIFTS), F32),
            pltpu.VMEM((secs, 2 * SHIFTS, cols * rows), BF16),
            pltpu.VMEM((3, 3, secs, 6 * cols, rows), BF16),
            pltpu.VMEM((3, 3, secs, cols, rows), F32),
            pltpu.VMEM((2, ext_secs, 2, 3 * cols, rows), F32),
            pltpu.VMEM((ext_secs, 4, 3 * cols, rows), F32),
            pltpu.VMEM((ext_secs, 3 * cols, rows), F32),
            pltpu.VMEM((ext_secs, 2, 3 * cols, rows), F32),
            pltpu.VMEM((ext_secs, 2, 3 * cols, rows), F32),
            dma((6 + secs,)),
            dma((secs, 2)), dma((secs, 2)),
            dma((3,)), dma((3,)),
            dma((4,)), dma((4,)),
            dma((4,)), dma((4,)),
        ],
        compiler_params=pltpu.CompilerParams(
            collective_id=0, has_side_effects=True, vmem_limit_bytes=63 * 2**20),
        name="align",
    )(pixels, valid.reshape(1, secs), offsets, neighbours, *consts)


def solution(mesh):
    return jax.shard_map(
        functools.partial(shards, mesh.shape["sec"], mesh.shape["tile"]),
        mesh=mesh,
        in_specs=(
            P("sec", "tile", None),
            P("sec", "tile"),
            P("sec", None, "tile", None),
            P("sec", None, "tile", None),
        ),
        out_specs=(P("sec", "tile", None, None), P("sec", None, "tile", None)),
        check_vma=False,
    )
```
